32 devices in a mesh: row: 8 (over y, x, core), frame: 4 (over z).
Axes of the slice: x: 2, y: 2, z: 4, core: 2. Of those that a mesh axis runs over, the one named last changes fastest.
Arguments:
- frames: bfloat16 [16, 64, 64, 128], P('frame', None, 'row'), may hold values from -6 to 6
- w_pair: bfloat16 [3, 3, 64, 128], replicated, may hold values from -0.1875 to 0.1875
- w_mixed: bfloat16 [3, 3, 64, 64], replicated, may hold values from -0.25 to 0.25
- slope_pair: float32 [64], replicated, may hold values from 0.05 to 0.5
- slope_mixed: float32 [64], replicated, may hold values from 0.05 to 0.5
Outputs:
- merged: bfloat16 [4, 64, 64, 128], P('frame', None, 'row')
The draws below stay inside these ranges and needn't reach their ends.
All inputs are finite; a program needn't handle non-finite values.
Results may differ from the reference program's by a relative error of at most 0.0051.
Values may be sent and summed in bfloat16 or wider, within the bound.
A program may use at most 64 MiB of HBM per device.

```python
import jax
import jax.numpy as jnp
from jax import lax

C = 64
W = 128
FRAMES = 16
H = 64


def shard_levels(stream_key, shape, cuts, smallest, top_value):
    loudness, own = 1.0, jax.random.fold_in(stream_key, 6)
    for axis_at, parts in cuts:
        steps = jnp.exp(jax.random.uniform(jax.random.fold_in(own, axis_at), (parts,), jnp.float32, smallest / len(cuts), top_value / len(cuts)))
        loudness = loudness * jnp.repeat(steps, shape[axis_at] // parts).reshape([-1 if axis == axis_at else 1 for axis in range(len(shape))])
    return loudness


def bell_draw(stream_key, extent, deviation, reach, shards=(), dtype=jnp.bfloat16):
    values = deviation * jax.random.normal(stream_key, extent, jnp.float32)
    if shards:
        values = values * shard_levels(stream_key, extent, shards, -0.22, 0.18)
    return jnp.clip(values, -reach, reach).astype(dtype)


def setup_inputs(seed: int = 0) -> dict:
    streams_of = jax.random.split(jax.random.key(seed), 6)
    frames = bell_draw(streams_of[0], (FRAMES, C, H, W), 1.0, 6.0, ((0, 4), (2, 8)))
    w_pair = bell_draw(streams_of[1], (3, 3, C, 2 * C), (18 * C) ** -0.5, 0.1875)
    w_mixed = bell_draw(streams_of[2], (3, 3, C, C), (9 * C) ** -0.5, 0.25)
    slope_pair = jnp.clip(jax.random.uniform(streams_of[3], (C,), jnp.float32, 0.05, 0.5), 0.05, 0.5)
    slope_mixed = jnp.clip(jax.random.uniform(streams_of[4], (C,), jnp.float32, 0.05, 0.5), 0.05, 0.5)
    return {"frames": frames, "w_pair": w_pair, "w_mixed": w_mixed, "slope_pair": slope_pair, "slope_mixed": slope_mixed}


def prelu(values, slope):
    return jnp.where(values >= 0, values, slope[:, None, None] * values)


def convolve(image, weight):
    rows = image.shape[1]
    cols = image.shape[2]
    padded = jnp.pad(image.astype(jnp.float32), ((0, 0), (1, 1), (1, 1)))
    wide = weight.astype(jnp.float32)
    total = jnp.zeros((weight.shape[2], rows, cols), jnp.float32)
    for tap_y in range(3):
        for tap_x in range(3):
            total = total + jnp.einsum("oc,chw->ohw", wide[tap_y, tap_x], padded[:, tap_y:tap_y + rows, tap_x:tap_x + cols], precision=lax.Precision.HIGHEST)
    return total


def merge_pair(first, second, w_pair, w_mixed, slope_pair, slope_mixed):
    joined = jnp.concatenate([first, second], axis=0)
    hidden = prelu(convolve(joined, w_pair), slope_pair).astype(jnp.bfloat16)
    branch = prelu(convolve(hidden, w_mixed), slope_mixed)
    return (first.astype(jnp.float32) + branch).astype(jnp.bfloat16)


def reference(frames, w_pair, w_mixed, slope_pair, slope_mixed):
    def apply(pair):
        return merge_pair(pair[0], pair[1], w_pair, w_mixed, slope_pair, slope_mixed)

    half = FRAMES // 2
    quarter = FRAMES // 4
    level_one = lax.map(apply, (frames[:half], frames[half:]))
    level_two = lax.map(apply, (level_one[:quarter], level_one[quarter:]))
    grouped = level_two.reshape(FRAMES // 16, 4, C, H, W)
    return jnp.transpose(grouped, (1, 0, 2, 3, 4)).reshape(quarter, C, H, W)
```

```python
import functools

import jax
import jax.numpy as jnp
from jax import lax
from jax.experimental import pallas as pl
from jax.experimental.pallas import tpu as pltpu
from jax.sharding import PartitionSpec as P

HALO = 4
GROUP = 4
TILE = 2


def spread(slope_ref, channels, cols):
    row = jnp.broadcast_to(slope_ref[...], (cols, channels))
    return row.T


def kernel(
    rows,
    cols,
    x_ref,
    w_pair_ref,
    w_mixed_ref,
    slope_pair_ref,
    slope_mixed_ref,
    out_ref,
    buf,
    acc,
    hidden,
    one,
    acc_two,
    wp,
    wm,
    sp,
    sm,
    send_z,
    recv_z,
    send_h,
    recv_h,
    own_sem,
):
    channels = x_ref.shape[1]
    row = lax.axis_index("row")
    place = lax.axis_index("frame")
    row_count = lax.axis_size("row")
    n = lax.axis_size("frame") // GROUP
    k = place // n
    m = place % n
    near = k + 1 - 2 * (k % 2)
    across = (k + 2) % GROUP
    far = GROUP - 1 - k
    has_up = row > 0
    has_down = row < row_count - 1
    edge = HALO * cols
    block = rows * cols

    def device(slot):
        return (row, slot * n + m)

    up = (row - 1, place)
    down = (row + 1, place)

    barrier = pltpu.get_barrier_semaphore()
    for slot in (near, across, far):
        pl.semaphore_signal(barrier, inc=1, device_id=device(slot), device_id_type=pl.DeviceIdType.MESH)

    @pl.when(has_up)
    def _():
        pl.semaphore_signal(barrier, inc=1, device_id=up, device_id_type=pl.DeviceIdType.MESH)

    @pl.when(has_down)
    def _():
        pl.semaphore_signal(barrier, inc=1, device_id=down, device_id_type=pl.DeviceIdType.MESH)

    pl.semaphore_wait(barrier, 3 + has_up.astype(jnp.int32) + has_down.astype(jnp.int32))

    def z_copy(slot):
        return pltpu.make_async_remote_copy(
            src_ref=x_ref.at[slot],
            dst_ref=buf.at[k, :, edge : edge + block],
            send_sem=send_z.at[slot],
            recv_sem=recv_z.at[k],
            device_id=device(slot),
            device_id_type=pl.DeviceIdType.MESH,
        )

    def z_arrival(slot):
        return pltpu.make_async_remote_copy(
            src_ref=x_ref.at[slot],
            dst_ref=buf.at[slot, :, edge : edge + block],
            send_sem=send_z.at[slot],
            recv_sem=recv_z.at[slot],
            device_id=device(slot),
            device_id_type=pl.DeviceIdType.MESH,
        )

    for slot in (far, across, near):
        z_copy(slot).start()

    def halo_up(slot):
        return pltpu.make_async_remote_copy(
            src_ref=buf.at[slot, :, edge : 2 * edge],
            dst_ref=buf.at[slot, :, edge + block : 2 * edge + block],
            send_sem=send_h.at[slot, 0],
            recv_sem=recv_h.at[slot, 0],
            device_id=up,
            device_id_type=pl.DeviceIdType.MESH,
        )

    def halo_down(slot):
        return pltpu.make_async_remote_copy(
            src_ref=buf.at[slot, :, block : block + edge],
            dst_ref=buf.at[slot, :, 0:edge],
            send_sem=send_h.at[slot, 1],
            recv_sem=recv_h.at[slot, 1],
            device_id=down,
            device_id_type=pl.DeviceIdType.MESH,
        )

    def forward(slot):
        @pl.when(has_up)
        def _():
            halo_up(slot).start()

        @pl.when(has_down)
        def _():
            halo_down(slot).start()

    def halo_wait(slot):
        @pl.when(has_up)
        def _():
            halo_down(slot).wait_recv()

        @pl.when(has_down)
        def _():
            halo_up(slot).wait_recv()

    own = pltpu.make_async_copy(x_ref.at[k], buf.at[k, :, edge : edge + block], own_sem)
    own.start()

    @pl.when(jnp.logical_not(has_up))
    def _():
        buf[:, :, 0:edge] = jnp.zeros((GROUP, channels, edge), buf.dtype)

    @pl.when(jnp.logical_not(has_down))
    def _():
        buf[:, :, edge + block : 2 * edge + block] = jnp.zeros((GROUP, channels, edge), buf.dtype)

    own.wait()
    forward(k)

    for kx in range(3):
        for part in range(2):
            wp[part, kx * channels : (kx + 1) * channels, :] = jnp.concatenate(
                [w_pair_ref[ky, kx][:, part * channels : (part + 1) * channels] for ky in range(3)], axis=1
            )
        wm[kx * channels : (kx + 1) * channels, :] = jnp.concatenate([w_mixed_ref[ky, kx] for ky in range(3)], axis=1)
    sp[...] = spread(slope_pair_ref, channels, cols)
    sm[...] = spread(slope_mixed_ref, channels, cols)

    lane = lax.broadcasted_iota(jnp.int32, (channels, cols), 1)
    not_first = lane > 0
    not_last = lane < cols - 1

    def tiles(count):
        return [(at, min(TILE, count - at)) for at in range(0, count, TILE)]

    def taps(weight, source, at, size):
        stacked = jnp.concatenate(
            [source[:, (at + ky) * cols : (at + ky + size) * cols] for ky in range(3)], axis=0
        )
        return jnp.dot(weight, stacked, preferred_element_type=jnp.float32)

    def joined(partial, i):
        left = partial[0:channels, i * cols : (i + 1) * cols]
        middle = partial[channels : 2 * channels, i * cols : (i + 1) * cols]
        right = partial[2 * channels :, i * cols : (i + 1) * cols]
        return (
            middle
            + jnp.where(not_first, pltpu.roll(left, 1, 1), 0.0)
            + jnp.where(not_last, pltpu.roll(right, cols - 1, 1), 0.0)
        )

    def prelu(values, slope):
        return jnp.where(values >= 0, values, slope[...] * values)

    def inside(values, image_row):
        if image_row < 0:
            return jnp.where(has_up, values, 0.0)
        if image_row >= rows:
            return jnp.where(has_down, values, 0.0)
        return values

    def begin(weight, source, target, reach):
        for at, size in tiles(rows + 2 * reach):
            target[:, at * cols : (at + size) * cols] = taps(weight, source, at, size)

    def merge(weight, source, started, first, first_reach, reach, target):
        for at, size in tiles(rows + 2 * reach + 2):
            partial = started[:, at * cols : (at + size) * cols] + taps(weight, source, at, size)
            for i in range(size):
                value = inside(prelu(joined(partial, i), sp), at + i - reach - 1)
                hidden[:, (at + i) * cols : (at + i + 1) * cols] = value.astype(hidden.dtype)
        weight_two = wm[...]
        for at, size in tiles(rows + 2 * reach):
            partial = taps(weight_two, hidden, at, size)
            for i in range(size):
                from_row = at + i - reach + first_reach
                base = first[:, from_row * cols : (from_row + 1) * cols].astype(jnp.float32)
                value = inside(base + prelu(joined(partial, i), sm), at + i - reach)
                target[:, (at + i) * cols : (at + i + 1) * cols] = value.astype(target.dtype)

    half = GROUP // 2

    def begin_pair(slot):
        begin(wp[slot // half], buf.at[slot], acc.at[slot % half], 3)

    def finish_pair(slot):
        pair = slot % half
        merge(wp[slot // half], buf.at[slot], acc.at[pair], buf.at[pair], HALO, 2, one.at[pair])

    halo_wait(k)
    begin_pair(k)
    z_arrival(near).wait_recv()
    forward(near)
    halo_wait(near)
    begin_pair(near)
    z_arrival(across).wait_recv()
    forward(across)
    z_arrival(far).wait_recv()
    forward(far)
    halo_wait(across)
    finish_pair(across)
    begin(wp[k % half], one.at[k % half], acc_two, 1)
    halo_wait(far)
    finish_pair(far)
    merge(wp[near % half], one.at[near % half], acc_two, one.at[0], 2, 0, out_ref)

    for slot in (near, across, far):
        z_copy(slot).wait_send()
    for slot in range(GROUP):
        @pl.when(has_up)
        def _():
            halo_up(slot).wait_send()

        @pl.when(has_down)
        def _():
            halo_down(slot).wait_send()


def on_device(frames, w_pair, w_mixed, slope_pair, slope_mixed):
    slots, channels, rows, cols = frames.shape
    x = frames.reshape(slots, channels, rows * cols)
    vmem = pl.BlockSpec(memory_space=pltpu.VMEM)
    wide = (rows + 2 * HALO) * cols
    merged = pl.pallas_call(
        functools.partial(kernel, rows, cols),
        out_shape=jax.ShapeDtypeStruct((channels, rows * cols), frames.dtype),
        in_specs=[vmem] * 5,
        out_specs=vmem,
        scratch_shapes=[
            pltpu.VMEM((GROUP, channels, wide), frames.dtype),
            pltpu.VMEM((2, 3 * channels, wide - 2 * cols), jnp.float32),
            pltpu.VMEM((channels, wide - 2 * cols), frames.dtype),
            pltpu.VMEM((2, channels, wide - 4 * cols), frames.dtype),
            pltpu.VMEM((3 * channels, wide - 6 * cols), jnp.float32),
            pltpu.VMEM((2, 3 * channels, 3 * channels), w_pair.dtype),
            pltpu.VMEM((3 * channels, 3 * channels), w_pair.dtype),
            pltpu.VMEM((channels, cols), jnp.float32),
            pltpu.VMEM((channels, cols), jnp.float32),
            pltpu.SemaphoreType.DMA((GROUP,)),
            pltpu.SemaphoreType.DMA((GROUP,)),
            pltpu.SemaphoreType.DMA((GROUP, 2)),
            pltpu.SemaphoreType.DMA((GROUP, 2)),
            pltpu.SemaphoreType.DMA,
        ],
        compiler_params=pltpu.CompilerParams(
            collective_id=0, has_side_effects=True, vmem_limit_bytes=32 * 1024 * 1024
        ),
    )(x, w_pair, w_mixed, slope_pair.reshape(1, channels), slope_mixed.reshape(1, channels))
    return merged.reshape(1, channels, rows, cols)


def solution(mesh):
    placed = (P("frame", None, "row", None), P(), P(), P(), P())
    return jax.shard_map(
        on_device,
        mesh=mesh,
        in_specs=placed,
        out_specs=P("frame", None, "row", None),
        check_vma=False,
    )
```

```python
import functools

import jax
import jax.numpy as jnp
from jax import lax
from jax.experimental import pallas as pl
from jax.experimental.pallas import tpu as pltpu
from jax.sharding import PartitionSpec as P

HALO = 4
GROUP = 4
TILE = 2
PIECES = 2


def spread(slope_ref, channels, cols):
    row = jnp.broadcast_to(slope_ref[...], (cols, channels))
    return row.T


def kernel(
    rows,
    cols,
    x_ref,
    w_pair_ref,
    w_mixed_ref,
    slope_pair_ref,
    slope_mixed_ref,
    out_ref,
    raw,
    x,
    w_pair_in,
    w_mixed_in,
    slope_pair_in,
    slope_mixed_in,
    buf,
    acc,
    hidden,
    one,
    acc_two,
    wp,
    wm,
    sp,
    sm,
    send_z,
    recv_z,
    send_h,
    recv_h,
    in_sem,
    w_sem,
):
    channels = x_ref.shape[1]
    row = lax.axis_index("row")
    place = lax.axis_index("frame")
    row_count = lax.axis_size("row")
    n = lax.axis_size("frame") // GROUP
    k = place // n
    m = place % n
    near = k + 1 - 2 * (k % 2)
    across = (k + 2) % GROUP
    far = GROUP - 1 - k
    has_up = row > 0
    has_down = row < row_count - 1
    edge = HALO
    deep = rows // PIECES

    def device(slot):
        return (row, slot * n + m)

    up = (row - 1, place)
    down = (row + 1, place)

    def fetch(slot):
        return pltpu.make_async_copy(x_ref.at[slot], raw.at[slot], in_sem.at[slot])

    def turned(slot):
        fetch(slot).wait()
        return jnp.swapaxes(raw[slot], 0, 1)

    loads = [
        pltpu.make_async_copy(source, target, w_sem.at[i])
        for i, (source, target) in enumerate(
            (
                (w_pair_ref, w_pair_in),
                (w_mixed_ref, w_mixed_in),
                (slope_pair_ref, slope_pair_in),
                (slope_mixed_ref, slope_mixed_in),
            )
        )
    ]
    for slot in (near, across, far, k):
        fetch(slot).start()

    barrier = pltpu.get_barrier_semaphore()
    for slot in (near, across, far):
        pl.semaphore_signal(barrier, inc=1, device_id=device(slot), device_id_type=pl.DeviceIdType.MESH)

    @pl.when(has_up)
    def _():
        pl.semaphore_signal(barrier, inc=1, device_id=up, device_id_type=pl.DeviceIdType.MESH)

    @pl.when(has_down)
    def _():
        pl.semaphore_signal(barrier, inc=1, device_id=down, device_id_type=pl.DeviceIdType.MESH)

    for load in loads:
        load.start()
    for slot in (near, across, far):
        x[slot] = turned(slot)
    pl.semaphore_wait(barrier, 3 + has_up.astype(jnp.int32) + has_down.astype(jnp.int32))

    def z_copy(slot, piece):
        return pltpu.make_async_remote_copy(
            src_ref=x.at[slot, piece * deep : (piece + 1) * deep],
            dst_ref=buf.at[k, edge + piece * deep : edge + (piece + 1) * deep],
            send_sem=send_z.at[slot, piece],
            recv_sem=recv_z.at[k, piece],
            device_id=device(slot),
            device_id_type=pl.DeviceIdType.MESH,
        )

    def z_arrival(slot, piece):
        return pltpu.make_async_remote_copy(
            src_ref=x.at[slot, piece * deep : (piece + 1) * deep],
            dst_ref=buf.at[slot, edge + piece * deep : edge + (piece + 1) * deep],
            send_sem=send_z.at[slot, piece],
            recv_sem=recv_z.at[slot, piece],
            device_id=device(slot),
            device_id_type=pl.DeviceIdType.MESH,
        )

    for piece in range(PIECES):
        for slot in (near, across, far):
            z_copy(slot, piece).start()

    def halo_up(slot):
        return pltpu.make_async_remote_copy(
            src_ref=buf.at[slot, edge : 2 * edge],
            dst_ref=buf.at[slot, edge + rows : 2 * edge + rows],
            send_sem=send_h.at[slot, 0],
            recv_sem=recv_h.at[slot, 0],
            device_id=up,
            device_id_type=pl.DeviceIdType.MESH,
        )

    def halo_down(slot):
        return pltpu.make_async_remote_copy(
            src_ref=buf.at[slot, rows : rows + edge],
            dst_ref=buf.at[slot, 0:edge],
            send_sem=send_h.at[slot, 1],
            recv_sem=recv_h.at[slot, 1],
            device_id=down,
            device_id_type=pl.DeviceIdType.MESH,
        )

    def forward(slot, piece):
        if piece == 0:
            @pl.when(has_up)
            def _():
                halo_up(slot).start()

        if piece == PIECES - 1:
            @pl.when(has_down)
            def _():
                halo_down(slot).start()

    def pass_on(slot, piece):
        z_arrival(slot, piece).wait_recv()
        forward(slot, piece)

    def halo_wait(slot):
        @pl.when(has_up)
        def _():
            halo_down(slot).wait_recv()

        @pl.when(has_down)
        def _():
            halo_up(slot).wait_recv()

    buf[k, edge : edge + rows] = turned(k)
    for piece in range(PIECES):
        forward(k, piece)

    @pl.when(jnp.logical_not(has_up))
    def _():
        buf[:, 0:edge] = jnp.zeros((GROUP, edge, channels, cols), buf.dtype)

    @pl.when(jnp.logical_not(has_down))
    def _():
        buf[:, edge + rows :] = jnp.zeros((GROUP, edge, channels, cols), buf.dtype)

    for load in loads:
        load.wait()

    for kx in range(3):
        for part in range(2):
            wp[part, kx * channels : (kx + 1) * channels, :] = jnp.concatenate(
                [w_pair_in[ky, kx][:, part * channels : (part + 1) * channels] for ky in range(3)], axis=1
            )
        wm[kx * channels : (kx + 1) * channels, :] = jnp.concatenate([w_mixed_in[ky, kx] for ky in range(3)], axis=1)
    sp[...] = spread(slope_pair_in, channels, cols)
    sm[...] = spread(slope_mixed_in, channels, cols)

    lane = lax.broadcasted_iota(jnp.int32, (channels, cols), 1)
    not_first = lane > 0
    not_last = lane < cols - 1

    def tiles(count):
        return [(at, min(TILE, count - at)) for at in range(0, count, TILE)]

    def taps(weight, source, at, size):
        lines = [source[at + i] for i in range(size + 2)]
        stacked = jnp.concatenate(
            [jnp.concatenate(lines[ky : ky + size], axis=1) for ky in range(3)], axis=0
        )
        return jnp.dot(weight, stacked, preferred_element_type=jnp.float32)

    def joined(partial, i):
        left = partial[0:channels, i * cols : (i + 1) * cols]
        middle = partial[channels : 2 * channels, i * cols : (i + 1) * cols]
        right = partial[2 * channels :, i * cols : (i + 1) * cols]
        return (
            middle
            + jnp.where(not_first, pltpu.roll(left, 1, 1), 0.0)
            + jnp.where(not_last, pltpu.roll(right, cols - 1, 1), 0.0)
        )

    def prelu(values, slope):
        return jnp.where(values >= 0, values, slope[...] * values)

    def inside(values, image_row):
        if image_row < 0:
            return jnp.where(has_up, values, 0.0)
        if image_row >= rows:
            return jnp.where(has_down, values, 0.0)
        return values

    def begin(weight, source, target, reach):
        for at, size in tiles(rows + 2 * reach):
            target[:, at * cols : (at + size) * cols] = taps(weight, source, at, size)

    def merge(weight, source, started, first, first_reach, reach, target):
        for at, size in tiles(rows + 2 * reach + 2):
            partial = started[:, at * cols : (at + size) * cols] + taps(weight, source, at, size)
            for i in range(size):
                value = inside(prelu(joined(partial, i), sp), at + i - reach - 1)
                hidden[at + i] = value.astype(hidden.dtype)
        weight_two = wm[...]
        for at, size in tiles(rows + 2 * reach):
            partial = taps(weight_two, hidden, at, size)
            for i in range(size):
                from_row = at + i - reach + first_reach
                base = first[from_row].astype(jnp.float32)
                value = inside(base + prelu(joined(partial, i), sm), at + i - reach)
                target[at + i] = value.astype(target.dtype)

    half = GROUP // 2

    def begin_pair(slot):
        begin(wp[slot // half], buf.at[slot], acc.at[slot % half], 3)

    def finish_pair(slot):
        pair = slot % half
        merge(wp[slot // half], buf.at[slot], acc.at[pair], buf.at[pair], HALO, 2, one.at[pair])

    halo_wait(k)
    begin_pair(k)
    for piece in range(PIECES - 1):
        for slot in (near, across, far):
            pass_on(slot, piece)
    pass_on(near, PIECES - 1)
    halo_wait(near)
    begin_pair(near)
    for slot in (across, far):
        pass_on(slot, PIECES - 1)
    halo_wait(across)
    finish_pair(across)
    begin(wp[k % half], one.at[k % half], acc_two, 1)
    halo_wait(far)
    finish_pair(far)
    merge(wp[near % half], one.at[near % half], acc_two, one.at[0], 2, 0, out_ref)

    for piece in range(PIECES):
        for slot in (near, across, far):
            z_copy(slot, piece).wait_send()
    for slot in range(GROUP):
        @pl.when(has_up)
        def _():
            halo_up(slot).wait_send()

        @pl.when(has_down)
        def _():
            halo_down(slot).wait_send()


def on_device(frames, w_pair, w_mixed, slope_pair, slope_mixed):
    slots, channels, rows, cols = frames.shape
    assert rows >= 2 * HALO
    slope_shape = (1, channels)
    vmem = pl.BlockSpec(memory_space=pltpu.VMEM)
    tall = rows + 2 * HALO
    merged = pl.pallas_call(
        functools.partial(kernel, rows, cols),
        out_shape=jax.ShapeDtypeStruct((rows, channels, cols), frames.dtype),
        in_specs=[pl.BlockSpec(memory_space=pltpu.HBM)] * 5,
        out_specs=vmem,
        scratch_shapes=[
            pltpu.VMEM(frames.shape, frames.dtype),
            pltpu.VMEM((slots, rows, channels, cols), frames.dtype),
            pltpu.VMEM(w_pair.shape, w_pair.dtype),
            pltpu.VMEM(w_mixed.shape, w_mixed.dtype),
            pltpu.VMEM(slope_shape, slope_pair.dtype),
            pltpu.VMEM(slope_shape, slope_mixed.dtype),
            pltpu.VMEM((GROUP, tall, channels, cols), frames.dtype),
            pltpu.VMEM((2, 3 * channels, (tall - 2) * cols), jnp.float32),
            pltpu.VMEM((tall - 2, channels, cols), frames.dtype),
            pltpu.VMEM((2, tall - 4, channels, cols), frames.dtype),
            pltpu.VMEM((3 * channels, (tall - 6) * cols), jnp.float32),
            pltpu.VMEM((2, 3 * channels, 3 * channels), w_pair.dtype),
            pltpu.VMEM((3 * channels, 3 * channels), w_pair.dtype),
            pltpu.VMEM((channels, cols), jnp.float32),
            pltpu.VMEM((channels, cols), jnp.float32),
            pltpu.SemaphoreType.DMA((GROUP, PIECES)),
            pltpu.SemaphoreType.DMA((GROUP, PIECES)),
            pltpu.SemaphoreType.DMA((GROUP, 2)),
            pltpu.SemaphoreType.DMA((GROUP, 2)),
            pltpu.SemaphoreType.DMA((GROUP,)),
            pltpu.SemaphoreType.DMA((4,)),
        ],
        compiler_params=pltpu.CompilerParams(
            collective_id=0, has_side_effects=True, vmem_limit_bytes=60 * 1024 * 1024
        ),
    )(frames, w_pair, w_mixed, slope_pair.reshape(slope_shape), slope_mixed.reshape(slope_shape))
    return merged.transpose(1, 0, 2)[None]


def solution(mesh):
    placed = (P("frame", None, "row", None), P(), P(), P(), P())
    return jax.shard_map(
        on_device,
        mesh=mesh,
        in_specs=placed,
        out_specs=P("frame", None, "row", None),
        check_vma=False,
    )
```

```python
import functools

import jax
import jax.numpy as jnp
from jax import lax
from jax.experimental import pallas as pl
from jax.experimental.pallas import tpu as pltpu
from jax.sharding import PartitionSpec as P

HALO = 4
GROUP = 4
TILE = 2
PIECES = 2


def spread(slope_ref, channels, cols):
    row = jnp.broadcast_to(slope_ref[...], (cols, channels))
    return row.T


def kernel(
    rows,
    cols,
    x_ref,
    w_pair_ref,
    w_mixed_ref,
    slope_pair_ref,
    slope_mixed_ref,
    out_ref,
    raw,
    x,
    w_pair_in,
    w_mixed_in,
    slope_pair_in,
    slope_mixed_in,
    buf,
    acc,
    hidden,
    one,
    acc_two,
    wp,
    wm,
    sp,
    sm,
    send_z,
    recv_z,
    send_h,
    recv_h,
    in_sem,
    w_sem,
):
    channels = x_ref.shape[1]
    row = lax.axis_index("row")
    place = lax.axis_index("frame")
    row_count = lax.axis_size("row")
    n = lax.axis_size("frame") // GROUP
    k = place // n
    m = place % n
    near = k + 1 - 2 * (k % 2)
    across = (k + 2) % GROUP
    far = GROUP - 1 - k
    has_up = row > 0
    has_down = row < row_count - 1
    edge = HALO
    deep = rows // PIECES

    def device(slot):
        return (row, slot * n + m)

    up = (row - 1, place)
    down = (row + 1, place)

    def fetch(slot):
        return pltpu.make_async_copy(x_ref.at[slot], raw.at[slot], in_sem.at[slot])

    def turned(slot):
        fetch(slot).wait()
        return jnp.swapaxes(raw[slot], 0, 1)

    loads = [
        pltpu.make_async_copy(source, target, w_sem.at[i])
        for i, (source, target) in enumerate(
            (
                (w_pair_ref, w_pair_in),
                (w_mixed_ref, w_mixed_in),
                (slope_pair_ref, slope_pair_in),
                (slope_mixed_ref, slope_mixed_in),
            )
        )
    ]
    for slot in (near, across, far, k):
        fetch(slot).start()

    barrier = pltpu.get_barrier_semaphore()
    for slot in (near, across, far):
        pl.semaphore_signal(barrier, inc=1, device_id=device(slot), device_id_type=pl.DeviceIdType.MESH)

    @pl.when(has_up)
    def _():
        pl.semaphore_signal(barrier, inc=1, device_id=up, device_id_type=pl.DeviceIdType.MESH)

    @pl.when(has_down)
    def _():
        pl.semaphore_signal(barrier, inc=1, device_id=down, device_id_type=pl.DeviceIdType.MESH)

    for load in loads:
        load.start()
    for slot in (near, across, far):
        x[slot] = turned(slot)
    buf[k, edge : edge + rows] = turned(k)
    pl.semaphore_wait(barrier, 3 + has_up.astype(jnp.int32) + has_down.astype(jnp.int32))

    def z_copy(slot, piece):
        return pltpu.make_async_remote_copy(
            src_ref=x.at[slot, piece * deep : (piece + 1) * deep],
            dst_ref=buf.at[k, edge + piece * deep : edge + (piece + 1) * deep],
            send_sem=send_z.at[slot, piece],
            recv_sem=recv_z.at[k, piece],
            device_id=device(slot),
            device_id_type=pl.DeviceIdType.MESH,
        )

    def z_arrival(slot, piece):
        return pltpu.make_async_remote_copy(
            src_ref=x.at[slot, piece * deep : (piece + 1) * deep],
            dst_ref=buf.at[slot, edge + piece * deep : edge + (piece + 1) * deep],
            send_sem=send_z.at[slot, piece],
            recv_sem=recv_z.at[slot, piece],
            device_id=device(slot),
            device_id_type=pl.DeviceIdType.MESH,
        )


    def halo_up(slot):
        return pltpu.make_async_remote_copy(
            src_ref=buf.at[slot, edge : 2 * edge],
            dst_ref=buf.at[slot, edge + rows : 2 * edge + rows],
            send_sem=send_h.at[slot, 0],
            recv_sem=recv_h.at[slot, 0],
            device_id=up,
            device_id_type=pl.DeviceIdType.MESH,
        )

    def halo_down(slot):
        return pltpu.make_async_remote_copy(
            src_ref=buf.at[slot, rows : rows + edge],
            dst_ref=buf.at[slot, 0:edge],
            send_sem=send_h.at[slot, 1],
            recv_sem=recv_h.at[slot, 1],
            device_id=down,
            device_id_type=pl.DeviceIdType.MESH,
        )

    def forward(slot, piece):
        if piece == 0:
            @pl.when(has_up)
            def _():
                halo_up(slot).start()

        if piece == PIECES - 1:
            @pl.when(has_down)
            def _():
                halo_down(slot).start()

    def pass_on(slot, piece):
        z_arrival(slot, piece).wait_recv()
        forward(slot, piece)

    def halo_wait(slot):
        @pl.when(has_up)
        def _():
            halo_down(slot).wait_recv()

        @pl.when(has_down)
        def _():
            halo_up(slot).wait_recv()

    for piece in range(1):
        for slot in (near, across, far):
            z_copy(slot, piece).start()
    for piece in range(PIECES):
        forward(k, piece)
    for piece in range(1, PIECES):
        for slot in (near, across, far):
            z_copy(slot, piece).start()

    @pl.when(jnp.logical_not(has_up))
    def _():
        buf[:, 0:edge] = jnp.zeros((GROUP, edge, channels, cols), buf.dtype)

    @pl.when(jnp.logical_not(has_down))
    def _():
        buf[:, edge + rows :] = jnp.zeros((GROUP, edge, channels, cols), buf.dtype)

    for load in loads:
        load.wait()

    for kx in range(3):
        for part in range(2):
            wp[part, kx * channels : (kx + 1) * channels, :] = jnp.concatenate(
                [w_pair_in[ky, kx][:, part * channels : (part + 1) * channels] for ky in range(3)], axis=1
            )
        wm[kx * channels : (kx + 1) * channels, :] = jnp.concatenate([w_mixed_in[ky, kx] for ky in range(3)], axis=1)
    sp[...] = spread(slope_pair_in, channels, cols)
    sm[...] = spread(slope_mixed_in, channels, cols)

    lane = lax.broadcasted_iota(jnp.int32, (channels, cols), 1)
    not_first = lane > 0
    not_last = lane < cols - 1

    def tiles(count):
        return [(at, min(TILE, count - at)) for at in range(0, count, TILE)]

    def taps(weight, source, at, size):
        lines = [source[at + i] for i in range(size + 2)]
        stacked = jnp.concatenate(
            [jnp.concatenate(lines[ky : ky + size], axis=1) for ky in range(3)], axis=0
        )
        return jnp.dot(weight, stacked, preferred_element_type=jnp.float32)

    def joined(partial, i):
        left = partial[0:channels, i * cols : (i + 1) * cols]
        middle = partial[channels : 2 * channels, i * cols : (i + 1) * cols]
        right = partial[2 * channels :, i * cols : (i + 1) * cols]
        return (
            middle
            + jnp.where(not_first, pltpu.roll(left, 1, 1), 0.0)
            + jnp.where(not_last, pltpu.roll(right, cols - 1, 1), 0.0)
        )

    def prelu(values, slope):
        return jnp.where(values >= 0, values, slope[...] * values)

    def inside(values, image_row):
        if image_row < 0:
            return jnp.where(has_up, values, 0.0)
        if image_row >= rows:
            return jnp.where(has_down, values, 0.0)
        return values

    def begin(weight, source, target, reach):
        for at, size in tiles(rows + 2 * reach):
            target[:, at * cols : (at + size) * cols] = taps(weight, source, at, size)

    def merge(weight, source, started, first, first_reach, reach, target):
        for at, size in tiles(rows + 2 * reach + 2):
            partial = started[:, at * cols : (at + size) * cols] + taps(weight, source, at, size)
            for i in range(size):
                value = inside(prelu(joined(partial, i), sp), at + i - reach - 1)
                hidden[at + i] = value.astype(hidden.dtype)
        weight_two = wm[...]
        for at, size in tiles(rows + 2 * reach):
            partial = taps(weight_two, hidden, at, size)
            for i in range(size):
                from_row = at + i - reach + first_reach
                base = first[from_row].astype(jnp.float32)
                value = inside(base + prelu(joined(partial, i), sm), at + i - reach)
                target[at + i] = value.astype(target.dtype)

    half = GROUP // 2

    def begin_pair(slot):
        begin(wp[slot // half], buf.at[slot], acc.at[slot % half], 3)

    def finish_pair(slot):
        pair = slot % half
        merge(wp[slot // half], buf.at[slot], acc.at[pair], buf.at[pair], HALO, 2, one.at[pair])

    halo_wait(k)
    begin_pair(k)
    for piece in range(PIECES - 1):
        for slot in (near, across, far):
            pass_on(slot, piece)
    pass_on(near, PIECES - 1)
    halo_wait(near)
    begin_pair(near)
    for slot in (across, far):
        pass_on(slot, PIECES - 1)
    halo_wait(across)
    finish_pair(across)
    begin(wp[k % half], one.at[k % half], acc_two, 1)
    halo_wait(far)
    finish_pair(far)
    merge(wp[near % half], one.at[near % half], acc_two, one.at[0], 2, 0, out_ref)

    for piece in range(PIECES):
        for slot in (near, across, far):
            z_copy(slot, piece).wait_send()
    for slot in range(GROUP):
        @pl.when(has_up)
        def _():
            halo_up(slot).wait_send()

        @pl.when(has_down)
        def _():
            halo_down(slot).wait_send()


def on_device(frames, w_pair, w_mixed, slope_pair, slope_mixed):
    slots, channels, rows, cols = frames.shape
    assert rows >= 2 * HALO
    slope_shape = (1, channels)
    vmem = pl.BlockSpec(memory_space=pltpu.VMEM)
    tall = rows + 2 * HALO
    merged = pl.pallas_call(
        functools.partial(kernel, rows, cols),
        out_shape=jax.ShapeDtypeStruct((rows, channels, cols), frames.dtype),
        in_specs=[pl.BlockSpec(memory_space=pltpu.HBM)] * 5,
        out_specs=vmem,
        scratch_shapes=[
            pltpu.VMEM(frames.shape, frames.dtype),
            pltpu.VMEM((slots, rows, channels, cols), frames.dtype),
            pltpu.VMEM(w_pair.shape, w_pair.dtype),
            pltpu.VMEM(w_mixed.shape, w_mixed.dtype),
            pltpu.VMEM(slope_shape, slope_pair.dtype),
            pltpu.VMEM(slope_shape, slope_mixed.dtype),
            pltpu.VMEM((GROUP, tall, channels, cols), frames.dtype),
            pltpu.VMEM((2, 3 * channels, (tall - 2) * cols), jnp.float32),
            pltpu.VMEM((tall - 2, channels, cols), frames.dtype),
            pltpu.VMEM((2, tall - 4, channels, cols), frames.dtype),
            pltpu.VMEM((3 * channels, (tall - 6) * cols), jnp.float32),
            pltpu.VMEM((2, 3 * channels, 3 * channels), w_pair.dtype),
            pltpu.VMEM((3 * channels, 3 * channels), w_pair.dtype),
            pltpu.VMEM((channels, cols), jnp.float32),
            pltpu.VMEM((channels, cols), jnp.float32),
            pltpu.SemaphoreType.DMA((GROUP, PIECES)),
            pltpu.SemaphoreType.DMA((GROUP, PIECES)),
            pltpu.SemaphoreType.DMA((GROUP, 2)),
            pltpu.SemaphoreType.DMA((GROUP, 2)),
            pltpu.SemaphoreType.DMA((GROUP,)),
            pltpu.SemaphoreType.DMA((4,)),
        ],
        compiler_params=pltpu.CompilerParams(
            collective_id=0, has_side_effects=True, vmem_limit_bytes=60 * 1024 * 1024
        ),
    )(frames, w_pair, w_mixed, slope_pair.reshape(slope_shape), slope_mixed.reshape(slope_shape))
    return merged.transpose(1, 0, 2)[None]


def solution(mesh):
    placed = (P("frame", None, "row", None), P(), P(), P(), P())
    return jax.shard_map(
        on_device,
        mesh=mesh,
        in_specs=placed,
        out_specs=P("frame", None, "row", None),
        check_vma=False,
    )
```
